32 devices in a mesh: rep: 8 (over z, core), tp: 4 (over y, x).
Axes of the slice: x: 2, y: 2, z: 4, core: 2. Of those that a mesh axis runs over, the one named last changes fastest.
Arguments:
- master: float32 [5120, 10240], P(('rep', 'tp')), may hold values from -0.078125 to 0.078125
- first_moment: float32 [5120, 10240], P(('rep', 'tp')), may hold values from -4 to 4
- second_moment: float32 [5120, 10240], P(('rep', 'tp')), may hold values from 0.1 to 4
- grads: bfloat16 [5120, 10240], P(('rep', 'tp')), may hold values from -6 to 6
- embed: bfloat16 [76800, 5120], P('rep', 'tp'), may hold values from -100 to 100
- ln_gain: float32 [5120], replicated, may hold values from 0.25 to 1.75
- post_gain: float32 [5120], replicated, may hold values from 0.25 to 1.75
- cache_keys: bfloat16 [512, 192, 1024], P('rep', None, 'tp'), may hold values from -600 to 600
- stored_values: bfloat16 [512, 192, 1024], P('rep', None, 'tp'), may hold values from -6 to 6
- lengths: int32 [512], P('rep'), may hold values from 2 to 192, as said below
- token_ids: int32 [512, 4], replicated, may hold values from 0 to 76799
Outputs:
- updated: float32 [5120, 10240], P(('rep', 'tp'))
- first: float32 [5120, 10240], P(('rep', 'tp'))
- second: float32 [5120, 10240], P(('rep', 'tp'))
- normed: bfloat16 [512, 4, 5120], P('rep', None, 'tp')
The draws below stay inside these ranges and needn't reach their ends.
Inputs may be any that keep to these rules, and one draw needn't show every extreme that they name: `lengths`: some row holds 192.
All inputs are finite; a program needn't handle non-finite values.
Results may differ from the reference program's by a relative error of at most 0.0034.
Values may be sent and summed in bfloat16 or wider, within the bound.
No kernel may reach another device: no remote copies, remote signals or barrier semaphores. Data moves between devices by JAX's collectives and lax.ppermute only.
A program may use at most 320 MiB of HBM per device.

```python
import math
import jax
import jax.numpy as jnp
import numpy as np
from jax import lax

MODEL_WIDTH = 5120
KEY_VALUE_HEADS = 8
HEAD_SIZE = 128
VOCAB = 76800
STEPS = 4
ROWS_REP = 64
CACHE_SLOTS = 192
QG = 4
GROUP_WIDTH = 1280
TOTAL_ROWS = 512


def draw_embed(key, part):
    key = jax.random.fold_in(key, 7)
    key_rows, key_jitter, key_base = jax.random.split(key, 3)
    row_scale = jnp.exp(jax.random.uniform(key_rows, (VOCAB, 1), jnp.float32, math.log(0.3), math.log(3.0)))
    position = jnp.arange(MODEL_WIDTH, dtype=jnp.float32)[None, :] / MODEL_WIDTH
    jitter = jnp.exp(jax.random.uniform(key_jitter, (1, MODEL_WIDTH), jnp.float32, 0.0, math.log(3.3)))
    column_scale = jnp.exp(math.log(3.0) * position) * jitter
    base = jnp.clip(jax.random.normal(key_base, (VOCAB, MODEL_WIDTH), jnp.float32), -6.0, 6.0)
    return (0.5 * base * row_scale * column_scale).astype(jnp.bfloat16)


def draw_cache_keys(key, part):
    key = jax.random.fold_in(key, 5)
    key_base = jax.random.fold_in(key, 0)
    array_shape = (TOTAL_ROWS, CACHE_SLOTS, KEY_VALUE_HEADS * HEAD_SIZE)
    values = jnp.clip(jax.random.normal(key_base, array_shape, jnp.float32), -6.0, 6.0)
    return values.astype(jnp.bfloat16)


def draw_lengths(key, part):
    key = jax.random.fold_in(key, 11)
    key_caps, key_rows, key_full = jax.random.split(key, 3)
    replicas = TOTAL_ROWS // ROWS_REP
    caps = jax.random.randint(key_caps, (replicas, 1), CACHE_SLOTS // 4, CACHE_SLOTS + 1)
    spread = jax.random.randint(key_rows, (replicas, ROWS_REP), 0, 1 << 20)
    drawn = 2 + spread % (caps - 1)
    drawn = drawn.reshape(TOTAL_ROWS)
    fullest = jax.random.randint(key_full, (), 0, TOTAL_ROWS)
    return jnp.where(jnp.arange(TOTAL_ROWS) == fullest, CACHE_SLOTS, drawn).astype(jnp.int32)


def touch_ends(values, key, low, high):
    index_at = [jax.random.randint(jax.random.fold_in(key, axis), (), 0, length) for axis, length in enumerate(values.shape)]
    widest = values.shape.index(max(values.shape))
    next_to = index_at[:widest] + [(index_at[widest] + 1) % values.shape[widest]] + index_at[widest + 1:]
    return values.at[tuple(index_at)].set(low).at[tuple(next_to)].set(high)


def shard_levels(rng, extent, cuts, least, top_value):
    level, own = 1.0, jax.random.fold_in(rng, 6)
    for dim, blocks in cuts:
        draws = jnp.exp(jax.random.uniform(jax.random.fold_in(own, dim), (blocks,), jnp.float32, least / len(cuts), top_value / len(cuts)))
        level = level * jnp.repeat(draws, extent[dim] // blocks).reshape([-1 if axis == dim else 1 for axis in range(len(extent))])
    return level


def wide_ids(own_key, shape, amount, skew):
    loads = [min(1 << octave, amount + 1 - (1 << octave)) * (1 << 20) // math.isqrt((1 << octave) ** skew) + 1 for octave in range((amount + 1).bit_length()) if 1 << octave <= amount]
    scale = 1 + sum(loads) // (1 << 30)
    table = np.cumsum(np.array([max(1, weight // scale) for weight in loads]))
    lot = jax.random.randint(jax.random.fold_in(own_key, 1), shape, 0, int(table[len(loads) - 1]))
    start = jnp.left_shift(1, jnp.searchsorted(jnp.asarray(table, jnp.int32), lot, side="right").astype(jnp.int32))
    grade = start - 1 + jax.random.randint(jax.random.fold_in(own_key, 4), shape, 0, 1 << 30) % jnp.minimum(start, amount + 1 - start)
    return jax.random.permutation(jax.random.fold_in(own_key, 2), amount)[grade].astype(jnp.int32)


def scatter_about(rng, dims, scale, most, cuts=(), held_as=jnp.bfloat16):
    values = jax.random.normal(rng, dims, jnp.float32) * scale
    if len(cuts) > 0:
        values = shard_levels(rng, dims, cuts, -0.22, 0.18) * values
    return jnp.clip(values, min=-most, max=most).astype(held_as)


def setup_inputs(seed: int = 0) -> dict:
    seeds = jax.random.split(jax.random.key(seed), 12)
    master = scatter_about(seeds[0], (MODEL_WIDTH, KEY_VALUE_HEADS * GROUP_WIDTH), MODEL_WIDTH ** -0.5, 0.078125, ((0, 32),), jnp.float32)
    first_moment = scatter_about(seeds[1], (MODEL_WIDTH, KEY_VALUE_HEADS * GROUP_WIDTH), 0.5, 4.0, ((0, 32),), jnp.float32)
    second_moment = jnp.clip(jnp.exp(math.log(4.0) - 3.6888794 * jax.random.uniform(seeds[2], (MODEL_WIDTH, KEY_VALUE_HEADS * GROUP_WIDTH), jnp.float32) ** shard_levels(seeds[2], (MODEL_WIDTH, KEY_VALUE_HEADS * GROUP_WIDTH), ((0, 32),), -0.2, 0.2)), 0.1, 4.0)
    grads = scatter_about(seeds[3], (MODEL_WIDTH, KEY_VALUE_HEADS * GROUP_WIDTH), 1.0, 6.0, ((0, 32),))
    embed = draw_embed(jax.random.fold_in(seeds[11], 71), 0)
    ln_gain = jnp.clip(1.0 + 0.15 * jax.random.normal(seeds[5], (MODEL_WIDTH,), jnp.float32), 0.25, 1.75)
    post_gain = jnp.clip(1.0 + 0.15 * jax.random.normal(seeds[6], (MODEL_WIDTH,), jnp.float32), 0.25, 1.75)
    cache_keys = draw_cache_keys(jax.random.fold_in(seeds[11], 71), 0)
    stored_values = scatter_about(seeds[8], (TOTAL_ROWS, CACHE_SLOTS, KEY_VALUE_HEADS * HEAD_SIZE), 1.0, 6.0, ((0, 8), (2, 4)))
    lengths = draw_lengths(jax.random.fold_in(seeds[11], 71), 0)
    token_ids = touch_ends(wide_ids(seeds[10], (TOTAL_ROWS, STEPS), VOCAB, 2), jax.random.fold_in(seeds[10], 3), 0, VOCAB - 1).astype(jnp.int32)
    return dict(master=master, first_moment=first_moment, second_moment=second_moment, grads=grads, embed=embed, ln_gain=ln_gain, post_gain=post_gain, cache_keys=cache_keys, stored_values=stored_values, lengths=lengths, token_ids=token_ids)


beta_one = 0.9
beta_two = 0.95
learn_rate = 0.001
adam_eps = 1e-08
norm_eps = 1e-06
correct_one = 1.0 - 0.9 ** 10
correct_two = 1.0 - 0.95 ** 10
masked_score = -1e+30

def rms_scale(values, gain):
    mean_sq = lax.optimization_barrier(jnp.mean(values * values, axis=-1, keepdims=True))
    return values * lax.rsqrt(mean_sq + norm_eps) * gain

def attend(queries, new_keys, new_values, keys, values, lengths):
    rows, steps, groups, qg, width = queries.shape
    keys = keys.reshape(rows, -1, groups, width).astype(jnp.float32)
    values = values.reshape(rows, -1, groups, width).astype(jnp.float32)
    places = keys.shape[1]
    scale = width ** (-0.5)
    qf = queries.astype(jnp.float32)
    cached = jnp.einsum('rsgqh,rcgh->rsgqc', qf, keys) * scale
    fresh = jnp.einsum('rsgqh,rtgh->rsgqt', qf, new_keys.astype(jnp.float32)) * scale
    live = jnp.arange(places, dtype=jnp.int32)[None, :] < lengths[:, None]
    cached = jnp.where(live[:, None, None, None, :], cached, masked_score)
    causal = jnp.arange(steps)[:, None] >= jnp.arange(steps)[None, :]
    fresh = jnp.where(causal[None, :, None, None, :], fresh, masked_score)
    top = jnp.maximum(lax.optimization_barrier(jnp.max(cached, axis=-1)), lax.optimization_barrier(jnp.max(fresh, axis=-1)))[..., None]
    cached = jnp.exp(cached - top)
    fresh = jnp.exp(fresh - top)
    total = lax.optimization_barrier(jnp.sum(cached, axis=-1, keepdims=True)) + lax.optimization_barrier(jnp.sum(fresh, axis=-1, keepdims=True))
    cached_w = (cached / total).astype(jnp.bfloat16).astype(jnp.float32)
    fresh_w = (fresh / total).astype(jnp.bfloat16).astype(jnp.float32)
    heads = jnp.einsum('rsgqc,rcgh->rsgqh', cached_w, values)
    heads = heads + jnp.einsum('rsgqt,rtgh->rsgqh', fresh_w, new_values.astype(jnp.float32))
    return heads.astype(jnp.bfloat16)

def reference(master, first_moment, second_moment, grads, embed, ln_gain, post_gain, cache_keys, stored_values, lengths, token_ids):
    slope = grads.astype(jnp.float32)
    first = beta_one * first_moment + (1.0 - beta_one) * slope
    second = beta_two * second_moment + (1.0 - beta_two) * slope * slope
    updated = master - learn_rate * (first / correct_one) / (jnp.sqrt(second / correct_two) + adam_eps)
    serving_replica = updated.astype(jnp.bfloat16)
    tokens = jnp.take(embed, token_ids.reshape(-1), axis=0)
    normed_in = rms_scale(tokens.astype(jnp.float32), ln_gain).astype(jnp.bfloat16)
    block_list = serving_replica.reshape(MODEL_WIDTH, KEY_VALUE_HEADS, GROUP_WIDTH)
    inner = (QG + 2) * HEAD_SIZE
    count = TOTAL_ROWS * STEPS
    attended = jnp.zeros((count, MODEL_WIDTH), jnp.float32)
    for head_group in range(KEY_VALUE_HEADS):
        projected = jnp.dot(normed_in, block_list[:, head_group, :inner], preferred_element_type=jnp.float32)
        projected = projected.astype(jnp.bfloat16).reshape(TOTAL_ROWS, STEPS, 1, inner)
        queries = projected[..., :QG * HEAD_SIZE].reshape(TOTAL_ROWS, STEPS, 1, QG, HEAD_SIZE)
        new_keys = projected[..., QG * HEAD_SIZE:(QG + 1) * HEAD_SIZE]
        new_values = projected[..., (QG + 1) * HEAD_SIZE:]
        keys = cache_keys[:, :, head_group * HEAD_SIZE:(head_group + 1) * HEAD_SIZE]
        values = stored_values[:, :, head_group * HEAD_SIZE:(head_group + 1) * HEAD_SIZE]
        heads = attend(queries, new_keys, new_values, keys, values, lengths)
        attended = attended + jnp.dot(heads.reshape(count, QG * HEAD_SIZE), block_list[:, head_group, inner:].T, preferred_element_type=jnp.float32)
    resid = tokens.astype(jnp.float32) + attended
    normed = rms_scale(resid, post_gain).astype(jnp.bfloat16).reshape(TOTAL_ROWS, STEPS, MODEL_WIDTH)
    return (updated, first, second, normed)
```

```python
import functools

import jax
import jax.numpy as jnp
from jax import lax
from jax.experimental import pallas as pl
from jax.experimental.pallas import tpu as pltpu
from jax.sharding import PartitionSpec as P

MODEL_WIDTH = 5120
HEAD_SIZE = 128
STEPS = 4
QG = 4
GROUP_WIDTH = 1280
INNER = (QG + 2) * HEAD_SIZE
OUTER = QG * HEAD_SIZE


beta_one = 0.9
beta_two = 0.95
learn_rate = 0.001
adam_eps = 1e-08
norm_eps = 1e-06
correct_one = 1.0 - 0.9**10
correct_two = 1.0 - 0.95**10
masked_score = -1e30


def adam_body(master, moment, variance, grads, updated, first, second, inner, outer):
    slope = grads[...].astype(jnp.float32)
    new_first = beta_one * moment[...] + (1.0 - beta_one) * slope
    new_second = beta_two * variance[...] + (1.0 - beta_two) * slope * slope
    new = master[...] - learn_rate * (new_first / correct_one) / (
        jnp.sqrt(new_second / correct_two) + adam_eps
    )
    first[...] = new_first
    second[...] = new_second
    updated[...] = new
    serving = new.astype(jnp.bfloat16)
    inner[0] = serving[:, :INNER]
    outer[0] = serving[:, INNER:]


def adam(master, moment, variance, grads, n_tp):
    rows, columns = master.shape
    groups = columns // GROUP_WIDTH
    local = groups // n_tp
    whole = pl.BlockSpec((rows, GROUP_WIDTH), lambda g: (0, g))
    part = lambda width: pl.BlockSpec((1, rows, width), lambda g: (g // local, 0, g % local))
    f32 = jax.ShapeDtypeStruct(master.shape, jnp.float32)
    return pl.pallas_call(
        adam_body,
        grid=(groups,),
        in_specs=[whole] * 4,
        out_specs=[whole] * 3 + [part(INNER), part(OUTER)],
        out_shape=[
            f32,
            f32,
            f32,
            jax.ShapeDtypeStruct((n_tp, rows, local * INNER), jnp.bfloat16),
            jax.ShapeDtypeStruct((n_tp, rows, local * OUTER), jnp.bfloat16),
        ],
        compiler_params=pltpu.CompilerParams(vmem_limit_bytes=40 * 2**20),
        cost_estimate=pl.CostEstimate(
            flops=15 * rows * columns, bytes_accessed=28 * rows * columns, transcendentals=0
        ),
    )(master, moment, variance, grads)


def attend(queries, new_keys, new_values, keys, values, lengths):
    rows, steps, groups, qg, width = queries.shape
    keys = keys.reshape(rows, -1, groups, width)
    values = values.reshape(rows, -1, groups, width)
    places = keys.shape[1]
    scale = width ** (-0.5)
    cached = (
        jnp.einsum("rsgqh,rcgh->rsgqc", queries, keys, preferred_element_type=jnp.float32) * scale
    )
    fresh = (
        jnp.einsum("rsgqh,rtgh->rsgqt", queries, new_keys, preferred_element_type=jnp.float32)
        * scale
    )
    live = jnp.arange(places, dtype=jnp.int32)[None, :] < lengths[:, None]
    cached = jnp.where(live[:, None, None, None, :], cached, masked_score)
    causal = jnp.arange(steps)[:, None] >= jnp.arange(steps)[None, :]
    fresh = jnp.where(causal[None, :, None, None, :], fresh, masked_score)
    top = jnp.maximum(jnp.max(cached, axis=-1), jnp.max(fresh, axis=-1))[..., None]
    cached = jnp.exp(cached - top)
    fresh = jnp.exp(fresh - top)
    total = jnp.sum(cached, axis=-1, keepdims=True) + jnp.sum(fresh, axis=-1, keepdims=True)
    cached_w = (cached / total).astype(jnp.bfloat16)
    fresh_w = (fresh / total).astype(jnp.bfloat16)
    heads = jnp.einsum("rsgqc,rcgh->rsgqh", cached_w, values, preferred_element_type=jnp.float32)
    heads = heads + jnp.einsum(
        "rsgqt,rtgh->rsgqh", fresh_w, new_values, preferred_element_type=jnp.float32
    )
    return heads.astype(jnp.bfloat16)


def flip(values, axis, bit):
    n = lax.axis_size(axis)
    return lax.ppermute(values, axis, [(i, i ^ bit) for i in range(n)])


def hop(values, first, last, step):
    pairs = [(2 * p + core, 2 * (p + step) + core) for p in range(first, last) for core in (0, 1)]
    return lax.ppermute(values, "rep", pairs)


def block_of(values, index):
    return lax.dynamic_index_in_dim(values, index, 0, keepdims=False)


def line_sum(blocks, plane, planes):
    right = left = None
    for step in range(1, planes):
        forth = block_of(blocks, jnp.minimum(plane + planes - step, planes - 1))
        back = block_of(blocks, jnp.maximum(plane - planes + step, 0))
        if right is not None:
            forth, back = forth + right, back + left
        right = hop(forth, 0, step, 1)
        left = hop(back, planes - step, planes, -1)
    return block_of(blocks, plane) + right + left


def line_gather(block, planes):
    right, left = [block], [block]
    for step in range(1, planes):
        right.append(hop(right[-1], step - 1, planes - 1, 1))
        left.append(hop(left[-1], 1, planes - step + 1, -1))
    return right, left


def shards(
    master,
    first_moment,
    second_moment,
    grads,
    embed,
    ln_gain,
    post_gain,
    cache_keys,
    stored_values,
    lengths,
    token_ids,
):
    n_rep = lax.axis_size("rep")
    n_tp = lax.axis_size("tp")
    rep, tp = lax.axis_index("rep"), lax.axis_index("tp")
    planes = n_rep // 2
    plane, core = rep // 2, rep % 2
    vocab_local, width_local = embed.shape
    rows_here = lengths.shape[0]
    count = rows_here * STEPS
    quarter = count // n_tp
    depth = MODEL_WIDTH // n_rep

    ids = token_ids.reshape(planes, 2, count)

    def lookup(which):
        local = block_of(ids.transpose(1, 0, 2), which) - rep * vocab_local
        inside = (local >= 0) & (local < vocab_local)
        found = jnp.take(embed, jnp.clip(local, 0, vocab_local - 1), axis=0)
        return jnp.where(inside[..., None], found, jnp.zeros_like(found))

    picked = flip(lookup(1 - core), "rep", 1) + lookup(core)
    own_cols = line_sum(picked, plane, planes)

    updated, first, second, inner, outer = adam(
        master, first_moment, second_moment, grads, n_tp
    )
    swap = lambda values: lax.all_to_all(values, "tp", split_axis=0, concat_axis=0, tiled=True)
    inner = swap(inner).reshape(depth, -1)
    outer = swap(outer).reshape(depth, -1)

    far = n_rep // 2
    masks, held = [0], [inner]
    bit = 2
    bits = []
    while bit < far:
        bits.append(bit)
        bit *= 2
    for bit in bits + [1]:
        masks = masks + [mask ^ bit for mask in masks]
        held = held + [flip(piece, "rep", bit) for piece in held]
    weights = jnp.concatenate(held, axis=0)

    tokens = swap(own_cols.reshape(n_tp, quarter, width_local)).astype(jnp.float32)
    mean_sq = jnp.sum(tokens * tokens, axis=(0, 2), keepdims=True) / MODEL_WIDTH
    normed_in = tokens * lax.rsqrt(mean_sq + norm_eps) * ln_gain.reshape(n_tp, 1, width_local)
    normed_in = normed_in.astype(jnp.bfloat16)

    def features_for(owner):
        parts = []
        for mask in masks:
            block = owner ^ mask
            at = (block // 2, 0, (block % 2) * depth)
            parts.append(lax.dynamic_slice(normed_in, at, (1, quarter, depth))[0])
        return jnp.concatenate(parts, axis=1)

    def all_tokens(values):
        spread = jnp.broadcast_to(values[None], (n_tp,) + values.shape)
        return swap(spread).reshape(count, -1)

    theirs = all_tokens(flip(features_for(rep ^ far), "rep", far))
    ours = all_tokens(features_for(rep))
    project = lambda x: jnp.dot(x, weights, preferred_element_type=jnp.float32)
    returned = flip(project(theirs).astype(jnp.bfloat16), "rep", far)
    projected = (project(ours) + returned.astype(jnp.float32)).astype(jnp.bfloat16)

    groups = projected.shape[1] // INNER
    projected = projected.reshape(rows_here, STEPS, groups, INNER)
    queries = projected[..., : QG * HEAD_SIZE].reshape(rows_here, STEPS, groups, QG, HEAD_SIZE)
    new_keys = projected[..., QG * HEAD_SIZE : (QG + 1) * HEAD_SIZE]
    new_values = projected[..., (QG + 1) * HEAD_SIZE :]
    heads = attend(queries, new_keys, new_values, cache_keys, stored_values, lengths)
    heads = heads.reshape(count, groups * OUTER)

    right, left = line_gather(outer, planes)

    def outward(*pieces):
        terms = [
            lax.dot_general(heads, w, (((1,), (1,)), ((), ())), preferred_element_type=jnp.float32)
            for w in pieces
        ]
        return functools.reduce(jnp.add, terms)

    partial_out = jnp.zeros((planes, count, width_local), jnp.bfloat16)
    for step in range(planes):
        pieces = [outer] if step == 0 else [right[step], left[planes - step]]
        mine = outward(*pieces)
        other = outward(*[flip(piece, "rep", 1) for piece in pieces])
        both = jnp.where(
            core == 0,
            jnp.concatenate([mine, other], axis=1),
            jnp.concatenate([other, mine], axis=1),
        ).astype(jnp.bfloat16)
        at = lax.rem(plane - step + planes, planes)
        partial_out = lax.dynamic_update_index_in_dim(partial_out, both, at, 0)
    attended = jnp.sum(swap(partial_out).astype(jnp.float32), axis=0)

    resid = own_cols.astype(jnp.float32) + attended
    square = jnp.sum(resid * resid, axis=-1)
    total = functools.reduce(
        jnp.add, [square] + [flip(square, "tp", other) for other in range(1, n_tp)]
    )
    gain = lax.dynamic_slice_in_dim(post_gain, tp * width_local, width_local, 0)
    normed = resid * lax.rsqrt(total / MODEL_WIDTH + norm_eps)[:, None] * gain
    normed = normed.astype(jnp.bfloat16).reshape(rows_here, STEPS, width_local)
    return (updated, first, second, normed)


def solution(mesh):
    return jax.shard_map(
        shards,
        mesh=mesh,
        in_specs=(
            P(("rep", "tp"), None),
            P(("rep", "tp"), None),
            P(("rep", "tp"), None),
            P(("rep", "tp"), None),
            P("rep", "tp"),
            P(),
            P(),
            P("rep", None, "tp"),
            P("rep", None, "tp"),
            P("rep"),
            P(),
        ),
        out_specs=(
            P(("rep", "tp"), None),
            P(("rep", "tp"), None),
            P(("rep", "tp"), None),
            P("rep", None, "tp"),
        ),
        check_vma=False,
    )
```

```python
import functools

import jax
import jax.numpy as jnp
from jax import lax
from jax.experimental import pallas as pl
from jax.experimental.pallas import tpu as pltpu
from jax.sharding import PartitionSpec as P

MODEL_WIDTH = 5120
HEAD_SIZE = 128
STEPS = 4
QG = 4
GROUP_WIDTH = 1280
INNER = (QG + 2) * HEAD_SIZE
OUTER = QG * HEAD_SIZE
SLOTS = 48
CHUNKS = 2


beta_one = 0.9
beta_two = 0.95
learn_rate = 0.001
adam_eps = 1e-08
norm_eps = 1e-06
correct_one = 1.0 - 0.9**10
correct_two = 1.0 - 0.95**10
masked_score = -1e30


def adam_body(master, moment, variance, grads, updated, first, second, inner, outer):
    slope = grads[...].astype(jnp.float32)
    new_first = beta_one * moment[...] + (1.0 - beta_one) * slope
    new_second = beta_two * variance[...] + (1.0 - beta_two) * slope * slope
    new = master[...] - learn_rate * (new_first / correct_one) / (
        jnp.sqrt(new_second / correct_two) + adam_eps
    )
    first[...] = new_first
    second[...] = new_second
    updated[...] = new
    serving = new.astype(jnp.bfloat16)
    inner[0] = serving[:, :INNER]
    outer[0] = serving[:, INNER:]


def adam(master, moment, variance, grads, n_tp):
    rows, columns = master.shape
    groups = columns // GROUP_WIDTH
    local = groups // n_tp
    whole = pl.BlockSpec((rows, GROUP_WIDTH), lambda g: (0, g))
    part = lambda width: pl.BlockSpec((1, rows, width), lambda g: (g // local, 0, g % local))
    f32 = jax.ShapeDtypeStruct(master.shape, jnp.float32)
    return pl.pallas_call(
        adam_body,
        grid=(groups,),
        in_specs=[whole] * 4,
        out_specs=[whole] * 3 + [part(INNER), part(OUTER)],
        out_shape=[
            f32,
            f32,
            f32,
            jax.ShapeDtypeStruct((n_tp, rows, local * INNER), jnp.bfloat16),
            jax.ShapeDtypeStruct((n_tp, rows, local * OUTER), jnp.bfloat16),
        ],
        compiler_params=pltpu.CompilerParams(vmem_limit_bytes=40 * 2**20),
        cost_estimate=pl.CostEstimate(
            flops=15 * rows * columns, bytes_accessed=28 * rows * columns, transcendentals=0
        ),
    )(master, moment, variance, grads)


def attend_body(lengths, queries, fresh_keys, fresh_values, keys, values, heads, *, block_row):
    rows, groups, lines, width = queries.shape
    places = keys.shape[1]
    scale = width ** (-0.5)
    start = block_row(pl.program_id(0)) * rows
    column = lax.broadcasted_iota(jnp.int32, (lines, places), 1)
    step_of = lax.broadcasted_iota(jnp.int32, (lines, lines), 0) // QG
    causal = lax.broadcasted_iota(jnp.int32, (lines, lines), 1) <= step_of
    across = (((1,), (1,)), ((), ()))
    scores = []
    for row in range(rows):
        live = column < lengths[start + row]
        for group in range(groups):
            at = slice(group * width, (group + 1) * width)
            query = queries[row, group]
            cached = lax.dot_general(
                query, keys[row, :, at], across, preferred_element_type=jnp.float32
            )
            fresh = lax.dot_general(
                query, fresh_keys[row, group], across, preferred_element_type=jnp.float32
            )
            cached = jnp.where(live, cached * scale, masked_score)
            fresh = jnp.where(causal, fresh * scale, masked_score)
            scores.append((cached, fresh))
    probs = []
    for cached, fresh in scores:
        top = jnp.maximum(
            jnp.max(cached, axis=-1, keepdims=True), jnp.max(fresh, axis=-1, keepdims=True)
        )
        cached = jnp.exp(cached - top)
        fresh = jnp.exp(fresh - top)
        total = jnp.sum(cached, axis=-1, keepdims=True) + jnp.sum(fresh, axis=-1, keepdims=True)
        probs.append(((cached / total).astype(jnp.bfloat16), (fresh / total).astype(jnp.bfloat16)))
    for row in range(rows):
        for group in range(groups):
            at = slice(group * width, (group + 1) * width)
            cached, fresh = probs[row * groups + group]
            out = jnp.dot(cached, values[row, :, at], preferred_element_type=jnp.float32)
            out = out + jnp.dot(
                fresh, fresh_values[row, group], preferred_element_type=jnp.float32
            )
            heads[row, group] = out.astype(jnp.bfloat16)


def attend(projected, keys, values, lengths, rows, chunk, chunks):
    count, columns = projected.shape
    groups = columns // INNER
    here = count // STEPS
    lines = STEPS * QG
    split = projected.reshape(here, STEPS, groups, INNER).transpose(0, 2, 1, 3)
    queries = split[..., :OUTER].reshape(here, groups, lines, HEAD_SIZE)
    pad = ((0, 0), (0, 0), (0, lines - STEPS), (0, 0))
    fresh_keys = jnp.pad(split[..., OUTER : OUTER + HEAD_SIZE], pad)
    fresh_values = jnp.pad(split[..., OUTER + HEAD_SIZE :], pad)
    places, width = keys.shape[1:]
    block_row = lambda i: i * chunks + chunk
    small = pl.BlockSpec((rows, groups, lines, HEAD_SIZE), lambda i, _: (i, 0, 0, 0))
    cache = pl.BlockSpec((rows, places, width), lambda i, _: (block_row(i), 0, 0))
    heads = pl.pallas_call(
        functools.partial(attend_body, block_row=block_row),
        grid_spec=pltpu.PrefetchScalarGridSpec(
            num_scalar_prefetch=1,
            grid=(here // rows,),
            in_specs=[small, small, small, cache, cache],
            out_specs=small,
        ),
        out_shape=jax.ShapeDtypeStruct(queries.shape, jnp.bfloat16),
        compiler_params=pltpu.CompilerParams(vmem_limit_bytes=32 * 2**20),
        cost_estimate=pl.CostEstimate(
            flops=4 * here * groups * lines * places * HEAD_SIZE,
            bytes_accessed=4 * here * places * width,
            transcendentals=here * groups * lines * places,
        ),
    )(lengths, queries, fresh_keys, fresh_values, keys, values)
    heads = heads.reshape(here, groups, STEPS, OUTER).transpose(0, 2, 1, 3)
    return heads.reshape(count, groups * OUTER)


def flip(values, axis, bit):
    n = lax.axis_size(axis)
    return lax.ppermute(values, axis, [(i, i ^ bit) for i in range(n)])


def hop(values, first, last, step):
    pairs = [(2 * p + core, 2 * (p + step) + core) for p in range(first, last) for core in (0, 1)]
    return lax.ppermute(values, "rep", pairs)


def block_of(values, index):
    return lax.dynamic_index_in_dim(values, index, 0, keepdims=False)


def line_sum(block, plane, planes):
    right = left = None
    for step in range(1, planes):
        forth = block(jnp.minimum(plane + planes - step, planes - 1))
        back = block(jnp.maximum(plane - planes + step, 0))
        if right is not None:
            forth, back = forth + right, back + left
        right = hop(forth.astype(jnp.bfloat16), 0, step, 1)
        left = hop(back.astype(jnp.bfloat16), planes - step, planes, -1)
    return block(plane) + right.astype(jnp.float32) + left.astype(jnp.float32)


def line_exchange(block, plane, planes):
    got = [block(plane)]
    for step in range(1, planes):
        right = hop(block(jnp.minimum(plane + step, planes - 1)), 0, planes - step, step)
        back = planes - step
        left = hop(block(jnp.maximum(plane - back, 0)), back, planes, -back)
        got.append(right + left)
    return got


def line_gather(block, planes):
    right, left = [block], [block]
    for step in range(1, planes):
        right.append(hop(right[-1], step - 1, planes - 1, 1))
        left.append(hop(left[-1], 1, planes - step + 1, -1))
    return [block] + [right[step] + left[planes - step] for step in range(1, planes)]


def find_rows(token_ids, embed, rep, tp, plane, core, planes):
    vocab_local, width = embed.shape
    ids = token_ids.reshape(2 * planes, -1)
    count = ids.shape[1]
    block = ids // vocab_local
    index = jnp.arange(count, dtype=jnp.int32)
    same = ids[:, :, None] == ids[:, None, :]
    leader = jnp.min(jnp.where(same, index[None, None, :], count), axis=2)
    first = leader == index[None, :]
    ahead = (block[:, :, None] == block[:, None, :]) & first[:, None, :]
    ahead = ahead & (index[None, None, :] < leader[:, :, None])
    number = jnp.sum(ahead.astype(jnp.int32), axis=2)
    rounds = jnp.max(number) // SLOTS + 1
    slots = jnp.arange(SLOTS, dtype=jnp.int32)
    listed = jnp.where(first & (block == rep), number, -1)
    my_block, my_number = block_of(block, rep), block_of(number, rep)
    behind = lax.rem(plane - my_block // 2 + planes, planes)
    cross = (my_block % 2 != core).astype(jnp.int32)
    base = (behind * 2 + cross) * SLOTS

    def one_round(turn):
        low = turn * SLOTS
        wanted = listed[:, :, None] == low + slots[None, None, :]
        local = jnp.where(wanted, (ids - rep * vocab_local)[:, :, None], 0)
        local = jnp.sum(local, axis=1).reshape(planes, 2, SLOTS)
        of_core = lambda c: lax.dynamic_index_in_dim(local, c, 1, keepdims=False)
        other = jnp.take(embed, of_core(1 - core), axis=0)
        other = flip(other, "rep", 1)
        mine = jnp.take(embed, of_core(core), axis=0)
        rows = jnp.concatenate([mine, other], axis=1)
        got = line_exchange(lambda d: block_of(rows, d), plane, planes)
        got = jnp.concatenate(got, axis=0)
        slot = my_number - low
        at = jnp.where((slot >= 0) & (slot < SLOTS), base + slot, -1)
        pick = (at[:, None] == jnp.arange(got.shape[0], dtype=jnp.int32)[None, :])
        found = jnp.dot(
            pick.astype(jnp.bfloat16), got, preferred_element_type=jnp.float32
        )
        return found.astype(jnp.bfloat16), rows

    found, rows = one_round(0)
    found = lax.fori_loop(1, rounds, lambda turn, kept: kept + one_round(turn)[0], found)
    return found, rows


def shards(
    master,
    first_moment,
    second_moment,
    grads,
    embed,
    ln_gain,
    post_gain,
    cache_keys,
    stored_values,
    lengths,
    token_ids,
):
    n_rep = lax.axis_size("rep")
    n_tp = lax.axis_size("tp")
    rep, tp = lax.axis_index("rep"), lax.axis_index("tp")
    planes = n_rep // 2
    plane, core = rep // 2, rep % 2
    width_local = embed.shape[1]
    rows_here = lengths.shape[0]
    count = rows_here * STEPS
    quarter = count // n_tp
    depth = MODEL_WIDTH // n_rep
    swap = lambda values: lax.all_to_all(values, "tp", split_axis=0, concat_axis=0, tiled=True)

    own_cols, rows = find_rows(token_ids, embed, rep, tp, plane, core, planes)

    master, rows = lax.optimization_barrier((master, rows))
    updated, first, second, inner, outer = adam(
        master, first_moment, second_moment, grads, n_tp
    )
    inner = swap(inner).reshape(depth, -1)
    outer = swap(outer).reshape(depth, -1)

    def both_cores(piece):
        pair = jnp.zeros((2,) + piece.shape, piece.dtype)
        pair = lax.dynamic_update_index_in_dim(pair, piece, core, 0)
        pair = lax.dynamic_update_index_in_dim(pair, flip(piece, "rep", 1), 1 - core, 0)
        return pair.reshape(-1, piece.shape[1])

    inner = both_cores(inner)

    gathered = line_gather(outer, planes)
    out_weights = jnp.zeros((planes, 2 * depth, outer.shape[1]), jnp.bfloat16)
    for step in range(planes):
        at = lax.rem(plane - step + planes, planes)
        out_weights = lax.dynamic_update_index_in_dim(
            out_weights, both_cores(gathered[step]), at, 0
        )

    tokens = swap(own_cols.reshape(n_tp, quarter, width_local)).astype(jnp.float32)
    mean_sq = jnp.sum(tokens * tokens, axis=(0, 2), keepdims=True) / MODEL_WIDTH
    normed_in = tokens * lax.rsqrt(mean_sq + norm_eps) * ln_gain.reshape(n_tp, 1, width_local)
    normed_in = normed_in.astype(jnp.bfloat16)

    chunks = CHUNKS
    piece = quarter // chunks
    gain = lax.dynamic_slice_in_dim(post_gain, tp * width_local, width_local, 0)
    own_cols = own_cols.reshape(n_tp, chunks, piece, width_local)
    outs = []
    for chunk in range(chunks):
        part = normed_in[:, chunk * piece : (chunk + 1) * piece]
        got = line_exchange(lambda d: block_of(part, d), plane, planes)
        spread = jnp.concatenate(got, axis=0)
        spread = swap(jnp.broadcast_to(spread[None], (n_tp,) + spread.shape))
        terms = jnp.dot(
            spread.reshape(-1, width_local), inner, preferred_element_type=jnp.float32
        ).reshape(n_tp, planes, piece, -1)

        def term(d):
            at = lax.rem(plane - d + planes, planes)
            found = lax.dynamic_index_in_dim(terms, at, 1, keepdims=False)
            return found.reshape(n_tp * piece, -1)

        projected = line_sum(term, plane, planes).astype(jnp.bfloat16)
        heads = attend(
            projected, cache_keys, stored_values, lengths, piece // STEPS, chunk, chunks
        )
        partial_out = jnp.stack(
            [
                lax.dot_general(
                    heads,
                    out_weights[at],
                    (((1,), (1,)), ((), ())),
                    preferred_element_type=jnp.float32,
                ).astype(jnp.bfloat16)
                for at in range(planes)
            ]
        )
        attended = jnp.sum(swap(partial_out).astype(jnp.float32), axis=0)
        resid = own_cols[:, chunk].reshape(n_tp * piece, -1).astype(jnp.float32) + attended
        square = jnp.sum(resid * resid, axis=-1)
        total = functools.reduce(
            jnp.add, [square] + [flip(square, "tp", other) for other in range(1, n_tp)]
        )
        normed = resid * lax.rsqrt(total / MODEL_WIDTH + norm_eps)[:, None] * gain
        outs.append(normed.astype(jnp.bfloat16).reshape(n_tp, piece, width_local))
    normed = jnp.stack(outs, axis=1).reshape(rows_here, STEPS, width_local)
    return (updated, first, second, normed)


def solution(mesh):
    return jax.shard_map(
        shards,
        mesh=mesh,
        in_specs=(
            P(("rep", "tp"), None),
            P(("rep", "tp"), None),
            P(("rep", "tp"), None),
            P(("rep", "tp"), None),
            P("rep", "tp"),
            P(),
            P(),
            P("rep", None, "tp"),
            P("rep", None, "tp"),
            P("rep"),
            P(),
        ),
        out_specs=(
            P(("rep", "tp"), None),
            P(("rep", "tp"), None),
            P(("rep", "tp"), None),
            P("rep", None, "tp"),
        ),
        check_vma=False,
    )
```

```python
import functools

import jax
import jax.numpy as jnp
from jax import lax
from jax.experimental import pallas as pl
from jax.experimental.pallas import tpu as pltpu
from jax.sharding import PartitionSpec as P

MODEL_WIDTH = 5120
HEAD_SIZE = 128
STEPS = 4
QG = 4
GROUP_WIDTH = 1280
INNER = (QG + 2) * HEAD_SIZE
OUTER = QG * HEAD_SIZE
SLOTS = 192
ROW_SLOTS = 48


beta_one = 0.9
beta_two = 0.95
learn_rate = 0.001
adam_eps = 1e-08
norm_eps = 1e-06
correct_one = 1.0 - 0.9**10
correct_two = 1.0 - 0.95**10
masked_score = -1e30


def adam_body(master, moment, variance, grads, *refs):
    updated, first, second, serving = refs[-4:]
    slope = grads[...].astype(jnp.float32)
    new_first = beta_one * moment[...] + (1.0 - beta_one) * slope
    new_second = beta_two * variance[...] + (1.0 - beta_two) * slope * slope
    new = master[...] - learn_rate * (new_first / correct_one) / (
        jnp.sqrt(new_second / correct_two) + adam_eps
    )
    first[...] = new_first
    second[...] = new_second
    updated[...] = new
    serving[0] = new.astype(jnp.bfloat16)


def adam(inputs, partial, n_tp, offset, width):
    rows, columns = inputs[0].shape
    groups = columns // GROUP_WIDTH
    local = groups // n_tp
    part = pl.BlockSpec(
        (pl.Element(rows), pl.Element(width)), lambda g: (0, pl.multiple_of(g * GROUP_WIDTH + offset, 256))
    )
    f32 = jax.ShapeDtypeStruct((rows, columns), jnp.float32)
    return pl.pallas_call(
        adam_body,
        grid=(groups,),
        in_specs=[part] * 4 + [pl.BlockSpec(memory_space=pl.ANY)] * len(partial),
        out_specs=[part] * 3
        + [pl.BlockSpec((1, rows, width), lambda g: (g // local, 0, g % local))],
        out_shape=[f32] * 3 + [jax.ShapeDtypeStruct((n_tp, rows, local * width), jnp.bfloat16)],
        input_output_aliases={4 + i: i for i in range(len(partial))},
        compiler_params=pltpu.CompilerParams(vmem_limit_bytes=56 * 2**20),
        cost_estimate=pl.CostEstimate(
            flops=15 * rows * groups * width,
            bytes_accessed=28 * rows * groups * width,
            transcendentals=0,
        ),
    )(*inputs, *partial)


BATCH = 96


def gather_body(ids, embed, out, blocks, stage, found, sems):
    batches = blocks.shape[0]

    def start(batch):
        def one(slot, carry):
            tile = pl.multiple_of((ids[batch * BATCH + slot] >> 4) * 16, 16)
            pltpu.make_async_copy(
                embed.at[pl.ds(tile, 16)],
                blocks.at[batch, pl.ds(pl.multiple_of(slot * 16, 16), 16)],
                sems.at[batch],
            ).start()
            return carry

        lax.fori_loop(0, BATCH, one, 0, unroll=8)

    def pick(batch):
        pltpu.make_async_copy(
            embed.at[pl.ds(0, BATCH * 16)], blocks.at[batch], sems.at[batch]
        ).wait()

        def some(turn, carry):
            for lane in range(8):
                slot = turn * 8 + lane
                tile = blocks[batch, pl.ds(pl.multiple_of(slot * 16, 16), 16)]
                stage[lane] = tile.astype(jnp.float32)
            for lane in range(8):
                slot = batch * BATCH + turn * 8 + lane
                found[pl.ds(slot, 1)] = stage[lane, pl.ds(ids[slot] & 15, 1)]
            return carry

        lax.fori_loop(0, BATCH // 8, some, 0)

    for batch in range(batches):
        start(batch)
    for batch in range(batches):
        pick(batch)
    out[...] = found[...].astype(out.dtype)


def gather_rows(embed, ids):
    slots, width = ids.shape[0], embed.shape[1]
    batches = slots // BATCH
    return pl.pallas_call(
        gather_body,
        grid_spec=pltpu.PrefetchScalarGridSpec(
            num_scalar_prefetch=1,
            grid=(1,),
            in_specs=[pl.BlockSpec(memory_space=pl.ANY)],
            out_specs=pl.BlockSpec((slots, width), lambda i, _: (0, 0)),
            scratch_shapes=[
                pltpu.VMEM((batches, BATCH * 16, width), embed.dtype),
                pltpu.VMEM((8, 16, width), jnp.float32),
                pltpu.VMEM((slots, width), jnp.float32),
                pltpu.SemaphoreType.DMA((batches,)),
            ],
        ),
        out_shape=jax.ShapeDtypeStruct((slots, width), embed.dtype),
        compiler_params=pltpu.CompilerParams(vmem_limit_bytes=56 * 2**20),
        cost_estimate=pl.CostEstimate(
            flops=0, bytes_accessed=40 * slots * width, transcendentals=0
        ),
    )(ids, embed)


def attend_body(lengths, queries, fresh_keys, fresh_values, keys, values, heads, *, block_row):
    rows, groups, lines, width = queries.shape
    places = keys.shape[1]
    scale = width ** (-0.5)
    start = block_row(pl.program_id(0)) * rows
    column = lax.broadcasted_iota(jnp.int32, (lines, places), 1)
    step_of = lax.broadcasted_iota(jnp.int32, (lines, lines), 0) // QG
    causal = lax.broadcasted_iota(jnp.int32, (lines, lines), 1) <= step_of
    across = (((1,), (1,)), ((), ()))
    scores = []
    for row in range(rows):
        live = column < lengths[start + row]
        for group in range(groups):
            at = slice(group * width, (group + 1) * width)
            query = queries[row, group]
            cached = lax.dot_general(
                query, keys[row, :, at], across, preferred_element_type=jnp.float32
            )
            fresh = lax.dot_general(
                query, fresh_keys[row, group], across, preferred_element_type=jnp.float32
            )
            cached = jnp.where(live, cached * scale, masked_score)
            fresh = jnp.where(causal, fresh * scale, masked_score)
            scores.append((cached, fresh))
    probs = []
    for cached, fresh in scores:
        top = jnp.maximum(
            jnp.max(cached, axis=-1, keepdims=True), jnp.max(fresh, axis=-1, keepdims=True)
        )
        cached = jnp.exp(cached - top)
        fresh = jnp.exp(fresh - top)
        total = jnp.sum(cached, axis=-1, keepdims=True) + jnp.sum(fresh, axis=-1, keepdims=True)
        probs.append(((cached / total).astype(jnp.bfloat16), (fresh / total).astype(jnp.bfloat16)))
    for row in range(rows):
        for group in range(groups):
            at = slice(group * width, (group + 1) * width)
            cached, fresh = probs[row * groups + group]
            out = jnp.dot(cached, values[row, :, at], preferred_element_type=jnp.float32)
            out = out + jnp.dot(
                fresh, fresh_values[row, group], preferred_element_type=jnp.float32
            )
            heads[row, group] = out.astype(jnp.bfloat16)


def attend(projected, keys, values, lengths, rows, chunk, chunks):
    count, columns = projected.shape
    groups = columns // INNER
    here = count // STEPS
    lines = STEPS * QG
    split = projected.reshape(here, STEPS, groups, INNER).transpose(0, 2, 1, 3)
    queries = split[..., :OUTER].reshape(here, groups, lines, HEAD_SIZE)
    pad = ((0, 0), (0, 0), (0, lines - STEPS), (0, 0))
    fresh_keys = jnp.pad(split[..., OUTER : OUTER + HEAD_SIZE], pad)
    fresh_values = jnp.pad(split[..., OUTER + HEAD_SIZE :], pad)
    places, width = keys.shape[1:]
    block_row = lambda i: i * chunks + chunk
    small = pl.BlockSpec((rows, groups, lines, HEAD_SIZE), lambda i, _: (i, 0, 0, 0))
    cache = pl.BlockSpec((rows, places, width), lambda i, _: (block_row(i), 0, 0))
    heads = pl.pallas_call(
        functools.partial(attend_body, block_row=block_row),
        grid_spec=pltpu.PrefetchScalarGridSpec(
            num_scalar_prefetch=1,
            grid=(here // rows,),
            in_specs=[small, small, small, cache, cache],
            out_specs=small,
        ),
        out_shape=jax.ShapeDtypeStruct(queries.shape, jnp.bfloat16),
        compiler_params=pltpu.CompilerParams(vmem_limit_bytes=56 * 2**20),
        cost_estimate=pl.CostEstimate(
            flops=4 * here * groups * lines * places * HEAD_SIZE,
            bytes_accessed=4 * here * places * width,
            transcendentals=here * groups * lines * places,
        ),
    )(lengths, queries, fresh_keys, fresh_values, keys, values)
    heads = heads.reshape(here, groups, STEPS, OUTER).transpose(0, 2, 1, 3)
    return heads.reshape(count, groups * OUTER)


def flip(values, axis, bit):
    n = lax.axis_size(axis)
    return lax.ppermute(values, axis, [(i, i ^ bit) for i in range(n)])


def hop(values, first, last, step):
    pairs = [(2 * p + core, 2 * (p + step) + core) for p in range(first, last) for core in (0, 1)]
    return lax.ppermute(values, "rep", pairs)


def block_of(values, index):
    return lax.dynamic_index_in_dim(values, index, 0, keepdims=False)


def line_sum(block, plane, planes):
    right = left = None
    for step in range(1, planes):
        forth = block(jnp.minimum(plane + planes - step, planes - 1))
        back = block(jnp.maximum(plane - planes + step, 0))
        if right is not None:
            forth, back = forth + right, back + left
        right = hop(forth.astype(jnp.bfloat16), 0, step, 1)
        left = hop(back.astype(jnp.bfloat16), planes - step, planes, -1)
    return block(plane) + right.astype(jnp.float32) + left.astype(jnp.float32)


def numbers(ids, block):
    count = ids.shape[-1]
    index = jnp.arange(count, dtype=jnp.int32)
    same = ids[..., :, None] == ids[..., None, :]
    leader = jnp.min(jnp.where(same, index[:, None], count), axis=-2)
    first = leader == index
    ahead = (block[..., :, None] == block[..., None, :]) & first[..., :, None]
    ahead = ahead & (index[:, None] < leader[..., None, :])
    return first, jnp.sum(ahead.astype(jnp.int32), axis=-2)


def listed(ids, chosen, number, low, slots):
    at = jnp.where(chosen, number - low, -1)
    hit = at[..., :, None] == jnp.arange(slots, dtype=jnp.int32)
    return jnp.sum(jnp.where(hit, ids[..., :, None], 0), axis=-2)


def placed(rows, block, number, low, slots):
    slot = number - low
    at = jnp.where((slot >= 0) & (slot < slots), block * slots + slot, -1)
    pick = at[:, None] == jnp.arange(rows.shape[0], dtype=jnp.int32)[None, :]
    return jnp.dot(pick.astype(jnp.bfloat16), rows, preferred_element_type=jnp.float32).astype(
        jnp.bfloat16
    )


def in_rounds(rounds, one_round):
    return lax.fori_loop(1, rounds, lambda turn, kept: kept + one_round(turn), one_round(0))


def shards(
    master,
    first_moment,
    second_moment,
    grads,
    embed,
    ln_gain,
    post_gain,
    cache_keys,
    stored_values,
    lengths,
    token_ids,
):
    n_rep = lax.axis_size("rep")
    n_tp = lax.axis_size("tp")
    rep, tp = lax.axis_index("rep"), lax.axis_index("tp")
    planes = n_rep // 2
    plane, core = rep // 2, rep % 2
    vocab_local, width_local = embed.shape
    rows_here = lengths.shape[0]
    count = rows_here * STEPS
    depth = MODEL_WIDTH // n_rep
    swap = lambda values, axis="tp": lax.all_to_all(
        values, axis, split_axis=0, concat_axis=0, tiled=True
    )

    weights_in = (master, first_moment, second_moment, grads)
    *partial, outer = adam(weights_in, (), n_tp, INNER, OUTER)
    outer = swap(outer).reshape(depth, -1)
    out_weights = lax.all_gather(outer, "rep", axis=0, tiled=True)

    token_ids, _ = lax.optimization_barrier((token_ids, partial[0]))
    ids = token_ids.reshape(n_rep, count)
    block = ids // vocab_local
    flat_ids, flat_block = ids.reshape(-1), block.reshape(-1)
    first, number = numbers(flat_ids, flat_block)
    core_tokens = lambda values: lax.dynamic_index_in_dim(
        values.reshape(planes, 2, count), core, 1, keepdims=False
    ).reshape(-1)
    core_block, core_number = core_tokens(flat_block), core_tokens(number)
    local_ids = flat_ids - rep * vocab_local

    def fetch(turn):
        return gather_rows(
            embed, listed(local_ids, first & (flat_block == rep), number, turn * SLOTS, SLOTS)
        )

    rows = fetch(0)
    held = lax.optimization_barrier((*weights_in, *partial, rows))
    updated, new_first, second, inner = adam(held[:4], held[4:7], n_tp, 0, INNER)
    inner = swap(inner).reshape(depth, -1)
    inner_other = flip(inner, "rep", 1)

    def normed_rows(turn):
        found = rows if isinstance(turn, int) else fetch(turn)
        tokens = swap(found.reshape(n_tp, -1, width_local)).astype(jnp.float32)
        mean_sq = jnp.sum(tokens * tokens, axis=(0, 2), keepdims=True) / MODEL_WIDTH
        normed_in = tokens * lax.rsqrt(mean_sq + norm_eps) * ln_gain.reshape(n_tp, 1, width_local)
        normed_in = normed_in.astype(jnp.bfloat16)
        share = normed_in.shape[1]
        normed_in = normed_in.reshape(n_tp, share, n_rep // n_tp, depth).transpose(0, 2, 1, 3)
        got = swap(normed_in.reshape(n_rep, share, depth), "rep")
        got = swap(jnp.broadcast_to(got[None], (n_tp,) + got.shape))
        got = got.transpose(1, 0, 2, 3).reshape(-1, depth)
        other = flip(got, "rep", 1)
        put = lambda values: placed(values, core_block, core_number, turn * SLOTS, SLOTS)
        return jnp.stack([put(got), put(other)])

    rounds = jnp.max(number) // SLOTS + 1
    spread = in_rounds(rounds, normed_rows)
    project = lambda x, w: jnp.dot(x, w, preferred_element_type=jnp.float32)
    terms = project(spread[0], inner) + project(spread[1], inner_other)
    terms = terms.reshape(planes, count, -1)
    projected = line_sum(lambda d: block_of(terms, d), plane, planes).astype(jnp.bfloat16)

    heads = attend(projected, cache_keys, stored_values, lengths, 8, 0, 1)

    row_first, row_number = numbers(ids, block)
    my_block, my_number = block_of(block, rep), block_of(row_number, rep)

    def own_rows(turn):
        low = turn * ROW_SLOTS
        wanted = listed(
            ids - rep * vocab_local, row_first & (block == rep), row_number, low, ROW_SLOTS
        )
        sent = gather_rows(embed, wanted.reshape(-1)).reshape(n_rep, ROW_SLOTS, width_local)
        got = swap(sent, "rep").reshape(-1, width_local)
        return placed(got, my_block, my_number, low, ROW_SLOTS)

    own_cols = in_rounds(jnp.max(row_number) // ROW_SLOTS + 1, own_rows)

    partial_out = jnp.stack(
        [
            lax.dot_general(
                heads,
                out_weights[at * width_local : (at + 1) * width_local],
                (((1,), (1,)), ((), ())),
                preferred_element_type=jnp.float32,
            ).astype(jnp.bfloat16)
            for at in range(n_tp)
        ]
    )
    attended = jnp.sum(swap(partial_out).astype(jnp.float32), axis=0)
    resid = own_cols.astype(jnp.float32) + attended
    square = jnp.sum(resid * resid, axis=-1)
    total = functools.reduce(
        jnp.add, [square] + [flip(square, "tp", other) for other in range(1, n_tp)]
    )
    gain = lax.dynamic_slice_in_dim(post_gain, tp * width_local, width_local, 0)
    normed = resid * lax.rsqrt(total / MODEL_WIDTH + norm_eps)[:, None] * gain
    normed = normed.astype(jnp.bfloat16).reshape(rows_here, STEPS, width_local)
    return (updated, new_first, second, normed)


def solution(mesh):
    return jax.shard_map(
        shards,
        mesh=mesh,
        in_specs=(
            P(("rep", "tp"), None),
            P(("rep", "tp"), None),
            P(("rep", "tp"), None),
            P(("rep", "tp"), None),
            P("rep", "tp"),
            P(),
            P(),
            P("rep", None, "tp"),
            P("rep", None, "tp"),
            P("rep"),
            P(),
        ),
        out_specs=(
            P(("rep", "tp"), None),
            P(("rep", "tp"), None),
            P(("rep", "tp"), None),
            P("rep", None, "tp"),
        ),
        check_vma=False,
    )
```

```python
import functools

import jax
import jax.numpy as jnp
from jax import lax
from jax.experimental import pallas as pl
from jax.experimental.pallas import tpu as pltpu
from jax.sharding import PartitionSpec as P

MODEL_WIDTH = 5120
HEAD_SIZE = 128
STEPS = 4
QG = 4
GROUP_WIDTH = 1280
INNER = (QG + 2) * HEAD_SIZE
OUTER = QG * HEAD_SIZE
SLOTS = 192
ROW_SLOTS = 48
PROJECT_STEPS = 2
ATTEND_ROWS = 8


beta_one = 0.9
beta_two = 0.95
learn_rate = 0.001
adam_eps = 1e-08
norm_eps = 1e-06
correct_one = 1.0 - 0.9**10
correct_two = 1.0 - 0.95**10
masked_score = -1e30


def adam_body(master, moment, variance, grads, *refs):
    updated, first, second, serving = refs[-4:]
    slope = grads[...].astype(jnp.float32)
    new_first = beta_one * moment[...] + (1.0 - beta_one) * slope
    new_second = beta_two * variance[...] + (1.0 - beta_two) * slope * slope
    new = master[...] - learn_rate * (new_first / correct_one) / (
        jnp.sqrt(new_second / correct_two) + adam_eps
    )
    first[...] = new_first
    second[...] = new_second
    updated[...] = new
    serving[0] = new.astype(jnp.bfloat16)


def adam(inputs, partial, n_tp, offset, width):
    rows, columns = inputs[0].shape
    groups = columns // GROUP_WIDTH
    local = groups // n_tp
    part = pl.BlockSpec(
        (pl.Element(rows), pl.Element(width)), lambda g: (0, pl.multiple_of(g * GROUP_WIDTH + offset, 256))
    )
    f32 = jax.ShapeDtypeStruct((rows, columns), jnp.float32)
    return pl.pallas_call(
        adam_body,
        grid=(groups,),
        in_specs=[part] * 4 + [pl.BlockSpec(memory_space=pl.ANY)] * len(partial),
        out_specs=[part] * 3
        + [pl.BlockSpec((1, rows, width), lambda g: (g // local, 0, g % local))],
        out_shape=[f32] * 3 + [jax.ShapeDtypeStruct((n_tp, rows, local * width), jnp.bfloat16)],
        input_output_aliases={4 + i: i for i in range(len(partial))},
        compiler_params=pltpu.CompilerParams(vmem_limit_bytes=56 * 2**20),
        cost_estimate=pl.CostEstimate(
            flops=15 * rows * groups * width,
            bytes_accessed=28 * rows * groups * width,
            transcendentals=0,
        ),
    )(*inputs, *partial)


BATCH = 96


def gather_body(ids, embed, out, blocks, stage, found, sems):
    batches = blocks.shape[0]

    def start(batch):
        def one(slot, carry):
            tile = pl.multiple_of((ids[batch * BATCH + slot] >> 4) * 16, 16)
            pltpu.make_async_copy(
                embed.at[pl.ds(tile, 16)],
                blocks.at[batch, pl.ds(pl.multiple_of(slot * 16, 16), 16)],
                sems.at[batch],
            ).start()
            return carry

        lax.fori_loop(0, BATCH, one, 0, unroll=8)

    def pick(batch):
        pltpu.make_async_copy(
            embed.at[pl.ds(0, BATCH * 16)], blocks.at[batch], sems.at[batch]
        ).wait()

        def some(turn, carry):
            for lane in range(8):
                slot = turn * 8 + lane
                tile = blocks[batch, pl.ds(pl.multiple_of(slot * 16, 16), 16)]
                stage[lane] = tile.astype(jnp.float32)
            for lane in range(8):
                slot = batch * BATCH + turn * 8 + lane
                found[pl.ds(slot, 1)] = stage[lane, pl.ds(ids[slot] & 15, 1)]
            return carry

        lax.fori_loop(0, BATCH // 8, some, 0)

    for batch in range(batches):
        start(batch)
    for batch in range(batches):
        pick(batch)
    out[...] = found[...].astype(out.dtype)


def gather_rows(embed, ids):
    slots, width = ids.shape[0], embed.shape[1]
    batches = slots // BATCH
    return pl.pallas_call(
        gather_body,
        grid_spec=pltpu.PrefetchScalarGridSpec(
            num_scalar_prefetch=1,
            grid=(1,),
            in_specs=[pl.BlockSpec(memory_space=pl.ANY)],
            out_specs=pl.BlockSpec((slots, width), lambda i, _: (0, 0)),
            scratch_shapes=[
                pltpu.VMEM((batches, BATCH * 16, width), embed.dtype),
                pltpu.VMEM((8, 16, width), jnp.float32),
                pltpu.VMEM((slots, width), jnp.float32),
                pltpu.SemaphoreType.DMA((batches,)),
            ],
        ),
        out_shape=jax.ShapeDtypeStruct((slots, width), embed.dtype),
        compiler_params=pltpu.CompilerParams(vmem_limit_bytes=56 * 2**20),
        cost_estimate=pl.CostEstimate(
            flops=0, bytes_accessed=40 * slots * width, transcendentals=0
        ),
    )(ids, embed)


def attend_body(lengths, fresh, keys, values, heads):
    rows, groups, _, width = fresh.shape
    lines, places = QG * STEPS, keys.shape[1]
    scale = width ** (-0.5)
    start = pl.program_id(0) * rows
    column = lax.broadcasted_iota(jnp.int32, (lines, places), 1)
    step_of = lax.broadcasted_iota(jnp.int32, (lines, 2 * STEPS), 0) % STEPS
    turn = lax.broadcasted_iota(jnp.int32, (lines, 2 * STEPS), 1) - STEPS
    causal = (turn >= 0) & (turn <= step_of)
    across = (((1,), (1,)), ((), ()))
    scores = []
    for row in range(rows):
        live = column < lengths[start + row]
        for group in range(groups):
            at = slice(group * width, (group + 1) * width)
            query = fresh[row, group, :lines]
            both = fresh[row, group, lines:]
            turned = pltpu.roll(both.astype(jnp.float32), STEPS, axis=0).astype(jnp.bfloat16)
            cached = lax.dot_general(
                query, keys[row, :, at], across, preferred_element_type=jnp.float32
            )
            new = lax.dot_general(query, turned, across, preferred_element_type=jnp.float32)
            cached = jnp.where(live, cached * scale, masked_score)
            new = jnp.where(causal, new * scale, masked_score)
            scores.append((cached, new, both))
    probs = []
    for cached, new, both in scores:
        top = jnp.maximum(
            jnp.max(cached, axis=-1, keepdims=True), jnp.max(new, axis=-1, keepdims=True)
        )
        cached = jnp.exp(cached - top)
        new = jnp.exp(new - top)
        total = jnp.sum(cached, axis=-1, keepdims=True) + jnp.sum(new, axis=-1, keepdims=True)
        probs.append(
            ((cached / total).astype(jnp.bfloat16), (new / total).astype(jnp.bfloat16), both)
        )
    for row in range(rows):
        for group in range(groups):
            at = slice(group * width, (group + 1) * width)
            cached, new, both = probs[row * groups + group]
            out = jnp.dot(cached, values[row, :, at], preferred_element_type=jnp.float32)
            out = out + jnp.dot(new, both, preferred_element_type=jnp.float32)
            heads[row, group] = out.astype(jnp.bfloat16)


def attend(projected, keys, values, lengths):
    count, columns = projected.shape
    groups = columns // INNER
    here = count // STEPS
    rows = min(ATTEND_ROWS, here)
    lines = STEPS * QG
    fresh = projected.reshape(here, STEPS, groups, QG + 2, HEAD_SIZE).transpose(0, 2, 3, 1, 4)
    fresh = fresh.reshape(here, groups, lines + 2 * STEPS, HEAD_SIZE)
    places, width = keys.shape[1:]
    cache = pl.BlockSpec((rows, places, width), lambda i, _: (i, 0, 0))
    heads = pl.pallas_call(
        attend_body,
        grid_spec=pltpu.PrefetchScalarGridSpec(
            num_scalar_prefetch=1,
            grid=(here // rows,),
            in_specs=[
                pl.BlockSpec((rows,) + fresh.shape[1:], lambda i, _: (i, 0, 0, 0)),
                cache,
                cache,
            ],
            out_specs=pl.BlockSpec((rows, groups, lines, HEAD_SIZE), lambda i, _: (i, 0, 0, 0)),
        ),
        out_shape=jax.ShapeDtypeStruct((here, groups, lines, HEAD_SIZE), jnp.bfloat16),
        compiler_params=pltpu.CompilerParams(vmem_limit_bytes=56 * 2**20),
        cost_estimate=pl.CostEstimate(
            flops=4 * here * groups * lines * places * HEAD_SIZE,
            bytes_accessed=4 * here * places * width,
            transcendentals=here * groups * lines * places,
        ),
    )(lengths, fresh, keys, values)
    heads = heads.reshape(here, groups, QG, STEPS, HEAD_SIZE).transpose(1, 2, 4, 0, 3)
    return heads.reshape(groups * OUTER, count)


def flip(values, axis, bit):
    n = lax.axis_size(axis)
    return lax.ppermute(values, axis, [(i, i ^ bit) for i in range(n)])


def hop(values, first, last, step):
    pairs = [(2 * p + core, 2 * (p + step) + core) for p in range(first, last) for core in (0, 1)]
    return lax.ppermute(values, "rep", pairs)


def block_of(values, index):
    return lax.dynamic_index_in_dim(values, index, 0, keepdims=False)


def outward_body(weights, heads, out):
    found = jnp.dot(weights[...], heads[...], preferred_element_type=jnp.float32)
    out[0] = found.astype(out.dtype)


def outward(weights, heads, n_tp):
    depth, count = heads.shape
    width = weights.shape[0] // n_tp
    return pl.pallas_call(
        outward_body,
        grid=(n_tp,),
        in_specs=[
            pl.BlockSpec((width, depth), lambda i: (i, 0)),
            pl.BlockSpec((depth, count), lambda i: (0, 0)),
        ],
        out_specs=pl.BlockSpec((1, width, count), lambda i: (i, 0, 0)),
        out_shape=jax.ShapeDtypeStruct((n_tp, width, count), jnp.bfloat16),
        compiler_params=pltpu.CompilerParams(vmem_limit_bytes=56 * 2**20),
        cost_estimate=pl.CostEstimate(
            flops=2 * count * depth * width * n_tp,
            bytes_accessed=2 * depth * width * n_tp,
            transcendentals=0,
        ),
    )(weights, heads)


def project_body(slots, here, there, inner_here, inner_there, out):
    rows = here.shape[0]
    column = lax.broadcasted_iota(jnp.int32, (slots.shape[0], rows), 1)
    pick = (column == slots[...]).astype(jnp.bfloat16)
    dot = functools.partial(jnp.dot, preferred_element_type=jnp.float32)
    first = dot(pick, here[...]).astype(jnp.bfloat16)
    second = dot(pick, there[...]).astype(jnp.bfloat16)
    out[...] = dot(first, inner_here[...]) + dot(second, inner_there[...])


def project(slots, here, there, inner_here, inner_there, planes):
    total = slots.shape[0]
    count = total // PROJECT_STEPS
    rows, depth = here.shape
    columns = inner_here.shape[1]
    all_of = lambda shape: pl.BlockSpec(shape, lambda i: (0, 0))
    return pl.pallas_call(
        project_body,
        grid=(PROJECT_STEPS,),
        in_specs=[pl.BlockSpec((count, 1), lambda i: (i, 0))]
        + [all_of((rows, depth))] * 2
        + [all_of((depth, columns))] * 2,
        out_specs=pl.BlockSpec((count, columns), lambda i: (i, 0)),
        out_shape=jax.ShapeDtypeStruct((total, columns), jnp.float32),
        compiler_params=pltpu.CompilerParams(vmem_limit_bytes=56 * 2**20),
        cost_estimate=pl.CostEstimate(
            flops=4 * total * depth * (rows + columns),
            bytes_accessed=4 * (rows + columns) * depth + 4 * total * columns,
            transcendentals=0,
        ),
    )(slots, here, there, inner_here, inner_there).reshape(planes, -1, columns)


def tie(values, *others):
    return lax.optimization_barrier((values, others))


def line_sum(block, plane, planes, late):
    right = left = None
    for step in range(1, planes):
        forth = block(jnp.minimum(plane + planes - step, planes - 1))
        back = block(jnp.maximum(plane - planes + step, 0))
        if right is not None:
            forth, back = forth + right, back + left
        right = hop(forth.astype(jnp.bfloat16), 0, step, 1)
        left = hop(back.astype(jnp.bfloat16), planes - step, planes, -1)
        if step == max(planes - 2, 1):
            (right, left), (late,) = tie((right, left), late)
    return block(plane) + right.astype(jnp.float32) + left.astype(jnp.float32), late


def leaders(ids):
    count = ids.shape[-1]
    index = jnp.arange(count, dtype=jnp.int32)
    same = ids[..., :, None] == ids[..., None, :]
    leader = jnp.min(jnp.where(same, index[:, None], count), axis=-2)
    return leader, leader == index


def numbers(block, leader, first):
    index = jnp.arange(block.shape[-1], dtype=jnp.int32)
    ahead = (block[..., :, None] == block[..., None, :]) & first[..., :, None]
    ahead = ahead & (index[:, None] < leader[..., None, :])
    return jnp.sum(ahead.astype(jnp.int32), axis=-2)


def listed(values, chosen, number, low, slots):
    at = jnp.where(chosen, number - low, -1)
    hit = at[..., :, None] == jnp.arange(slots, dtype=jnp.int32)
    return jnp.sum(jnp.where(hit, values[..., :, None], 0), axis=-2)


def slot_of(block, number, low, slots):
    slot = number - low
    return jnp.where((slot >= 0) & (slot < slots), block * slots + slot, -1)


def picked(slot, rows):
    pick = slot[:, None] == jnp.arange(rows.shape[0], dtype=jnp.int32)[None, :]
    return jnp.dot(pick.astype(jnp.bfloat16), rows, preferred_element_type=jnp.float32).astype(
        jnp.bfloat16
    )


def exchange(blocks, axis, place):
    n = blocks.shape[0]
    out = lax.dynamic_update_index_in_dim(blocks, block_of(blocks, place), place, 0)
    for mask in range(1, n):
        got = flip(block_of(blocks, place ^ mask), axis, mask)
        out = lax.dynamic_update_index_in_dim(out, got, place ^ mask, 0)
    return out


def shards(
    master,
    first_moment,
    second_moment,
    grads,
    embed,
    ln_gain,
    post_gain,
    cache_keys,
    stored_values,
    lengths,
    token_ids,
):
    n_rep = lax.axis_size("rep")
    n_tp = lax.axis_size("tp")
    rep, tp = lax.axis_index("rep"), lax.axis_index("tp")
    planes = n_rep // 2
    plane, core = rep // 2, rep % 2
    vocab_local, width_local = embed.shape
    rows_here = lengths.shape[0]
    count = rows_here * STEPS
    depth = MODEL_WIDTH // n_rep
    swap = lambda values, axis="tp": lax.all_to_all(
        values, axis, split_axis=0, concat_axis=0, tiled=True
    )

    ids = token_ids.reshape(n_rep, count)
    block = ids // vocab_local
    flat_ids, flat_block = ids.reshape(-1), block.reshape(-1)
    leader, first = leaders(flat_ids)
    mine = first & (flat_block == rep)
    index = jnp.arange(flat_ids.shape[0], dtype=jnp.int32)
    place = jnp.sum((mine[:, None] & (index[:, None] < index[None, :])).astype(jnp.int32), axis=0)
    local_ids = flat_ids - rep * vocab_local
    fetch = lambda turn: gather_rows(embed, listed(local_ids, mine, place, turn * SLOTS, SLOTS))
    rows = fetch(0)
    swapped = swap(rows.reshape(n_tp, -1, width_local))

    weights_in = (master, first_moment, second_moment, grads)
    weights_in, _ = tie(weights_in, rows)
    *partial, outer = adam(weights_in, (), n_tp, INNER, OUTER)
    swapped, (outer,) = tie(swapped, outer)
    outer = exchange(outer, "tp", tp).reshape(depth, -1)
    out_weights = lax.all_gather(outer, "rep", axis=0, tiled=True)

    def normed_rows(found):
        tokens = found.astype(jnp.float32)
        mean_sq = jnp.sum(tokens * tokens, axis=(0, 2), keepdims=True) / MODEL_WIDTH
        normed_in = tokens * lax.rsqrt(mean_sq + norm_eps) * ln_gain.reshape(n_tp, 1, width_local)
        normed_in = normed_in.astype(jnp.bfloat16)
        share = normed_in.shape[1]
        normed_in = normed_in.reshape(n_tp, share, n_rep // n_tp, depth).transpose(0, 2, 1, 3)
        return normed_in.reshape(n_rep, share, depth)

    def all_slots(got):
        got = swap(jnp.broadcast_to(got[None], (n_tp,) + got.shape))
        return got.transpose(1, 0, 2, 3).reshape(-1, depth)

    normed_in = normed_rows(swapped)
    got = swap(normed_in, "rep")
    (weights_in, partial), _ = tie((weights_in, partial), normed_in)
    updated, new_first, second, inner = adam(weights_in, partial, n_tp, 0, INNER)
    got, (inner,) = tie(got, inner)
    inner = exchange(inner, "tp", tp).reshape(depth, -1)
    got, (inner,) = tie(got, inner)
    inner_other = flip(inner, "rep", 1)

    here = all_slots(got)
    flat_block, _ = tie(flat_block, got)
    number = numbers(flat_block, leader, first)
    core_tokens = lambda values: lax.dynamic_index_in_dim(
        values.reshape(planes, 2, count), core, 1, keepdims=False
    ).reshape(-1)
    core_block, core_number = core_tokens(flat_block), core_tokens(number)
    rounds = jnp.max(number) // SLOTS + 1

    def terms_of(here, turn):
        slot = slot_of(core_block, core_number, turn * SLOTS, SLOTS)
        return project(slot[:, None], here, flip(here, "rep", 1), inner, inner_other, planes)

    def terms_again(turn):
        found = swap(fetch(turn).reshape(n_tp, -1, width_local))
        return terms_of(all_slots(swap(normed_rows(found), "rep")), turn)

    terms = terms_of(here, 0)
    terms = lax.fori_loop(1, rounds, lambda turn, kept: kept + terms_again(turn), terms)

    ids, _ = tie(ids, terms)
    row_leader, row_first = leaders(ids)
    row_number = numbers(block, row_leader, row_first)
    my_block, my_number = block_of(block, rep), block_of(row_number, rep)

    def to_send(far, near, found):
        low = far * ROW_SLOTS
        chosen = row_first & (block == rep)
        of = listed(number.reshape(n_rep, -1) + 1, chosen, row_number, low, ROW_SLOTS)
        slot = slot_of(0, of.reshape(-1) - 1, near * SLOTS, SLOTS)
        return picked(slot, found).reshape(n_rep, ROW_SLOTS, width_local)

    def own_rows(far, sent):
        found = swap(sent, "rep").reshape(-1, width_local)
        return picked(slot_of(my_block, my_number, far * ROW_SLOTS, ROW_SLOTS), found)

    sent = to_send(0, 0, rows)
    projected, (out_weights, sent) = line_sum(
        lambda d: block_of(terms, d), plane, planes, (out_weights, sent)
    )
    projected = projected.astype(jnp.bfloat16)
    sent, _ = tie(sent, projected)
    own_cols = own_rows(0, sent)

    heads = attend(projected, cache_keys, stored_values, lengths)
    heads, (own_cols,) = tie(heads, own_cols)
    own_cols = lax.fori_loop(
        1,
        (jnp.max(row_number) // ROW_SLOTS + 1) * rounds,
        lambda turn, kept: kept
        + own_rows(
            turn // rounds, to_send(turn // rounds, turn % rounds, fetch(turn % rounds))
        ),
        own_cols,
    )

    partial_out = outward(out_weights, heads, n_tp)
    attended = jnp.sum(swap(partial_out).astype(jnp.float32), axis=0).T
    resid = own_cols.astype(jnp.float32) + attended
    square = jnp.sum(resid * resid, axis=-1)
    total = functools.reduce(
        jnp.add, [square] + [flip(square, "tp", other) for other in range(1, n_tp)]
    )
    gain = lax.dynamic_slice_in_dim(post_gain, tp * width_local, width_local, 0)
    normed = resid * lax.rsqrt(total / MODEL_WIDTH + norm_eps)[:, None] * gain
    normed = normed.astype(jnp.bfloat16).reshape(rows_here, STEPS, width_local)
    return (updated, new_first, second, normed)


def solution(mesh):
    return jax.shard_map(
        shards,
        mesh=mesh,
        in_specs=(
            P(("rep", "tp"), None),
            P(("rep", "tp"), None),
            P(("rep", "tp"), None),
            P(("rep", "tp"), None),
            P("rep", "tp"),
            P(),
            P(),
            P("rep", None, "tp"),
            P("rep", None, "tp"),
            P("rep"),
            P(),
        ),
        out_specs=(
            P(("rep", "tp"), None),
            P(("rep", "tp"), None),
            P(("rep", "tp"), None),
            P("rep", None, "tp"),
        ),
        check_vma=False,
    )
```

```python
import functools

import jax
import jax.numpy as jnp
from jax import lax
from jax.experimental import pallas as pl
from jax.experimental.pallas import tpu as pltpu
from jax.sharding import PartitionSpec as P

MODEL_WIDTH = 5120
HEAD_SIZE = 128
STEPS = 4
QG = 4
GROUP_WIDTH = 1280
INNER = (QG + 2) * HEAD_SIZE
OUTER = QG * HEAD_SIZE
SLOTS = 192
ROW_SLOTS = 48
PROJECT_STEPS = 2
ATTEND_ROWS = 16
SUM_PARTS = 2


beta_one = 0.9
beta_two = 0.95
learn_rate = 0.001
adam_eps = 1e-08
norm_eps = 1e-06
correct_one = 1.0 - 0.9**10
correct_two = 1.0 - 0.95**10
masked_score = -1e30


def adam_body(master, moment, variance, grads, *refs):
    updated, first, second, serving = refs[-4:]
    slope = grads[...].astype(jnp.float32)
    new_first = beta_one * moment[...] + (1.0 - beta_one) * slope
    new_second = beta_two * variance[...] + (1.0 - beta_two) * slope * slope
    new = master[...] - learn_rate * (new_first / correct_one) / (
        jnp.sqrt(new_second / correct_two) + adam_eps
    )
    first[...] = new_first
    second[...] = new_second
    updated[...] = new
    serving[0] = new.astype(jnp.bfloat16)


def adam(inputs, partial, n_tp, offset, width):
    rows, columns = inputs[0].shape
    groups = columns // GROUP_WIDTH
    local = groups // n_tp
    part = pl.BlockSpec(
        (pl.Element(rows), pl.Element(width)), lambda g: (0, pl.multiple_of(g * GROUP_WIDTH + offset, 256))
    )
    f32 = jax.ShapeDtypeStruct((rows, columns), jnp.float32)
    return pl.pallas_call(
        adam_body,
        grid=(groups,),
        in_specs=[part] * 4 + [pl.BlockSpec(memory_space=pl.ANY)] * len(partial),
        out_specs=[part] * 3
        + [pl.BlockSpec((1, rows, width), lambda g: (g // local, 0, g % local))],
        out_shape=[f32] * 3 + [jax.ShapeDtypeStruct((n_tp, rows, local * width), jnp.bfloat16)],
        input_output_aliases={4 + i: i for i in range(len(partial))},
        compiler_params=pltpu.CompilerParams(vmem_limit_bytes=56 * 2**20),
        cost_estimate=pl.CostEstimate(
            flops=15 * rows * groups * width,
            bytes_accessed=28 * rows * groups * width,
            transcendentals=0,
        ),
    )(*inputs, *partial)


BATCH = 96


def gather_body(ids, embed, out, blocks, stage, found, sems):
    batches = blocks.shape[0]

    def start(batch):
        def one(slot, carry):
            tile = pl.multiple_of((ids[batch * BATCH + slot] >> 4) * 16, 16)
            pltpu.make_async_copy(
                embed.at[pl.ds(tile, 16)],
                blocks.at[batch, pl.ds(pl.multiple_of(slot * 16, 16), 16)],
                sems.at[batch],
            ).start()
            return carry

        lax.fori_loop(0, BATCH, one, 0, unroll=8)

    def pick(batch):
        pltpu.make_async_copy(
            embed.at[pl.ds(0, BATCH * 16)], blocks.at[batch], sems.at[batch]
        ).wait()

        def some(turn, carry):
            for lane in range(8):
                slot = turn * 8 + lane
                tile = blocks[batch, pl.ds(pl.multiple_of(slot * 16, 16), 16)]
                stage[lane] = tile.astype(jnp.float32)
            for lane in range(8):
                slot = batch * BATCH + turn * 8 + lane
                found[pl.ds(slot, 1)] = stage[lane, pl.ds(ids[slot] & 15, 1)]
            return carry

        lax.fori_loop(0, BATCH // 8, some, 0)

    for batch in range(batches):
        start(batch)
    for batch in range(batches):
        pick(batch)
    out[...] = found[...].astype(out.dtype)


def gather_rows(embed, ids):
    slots, width = ids.shape[0], embed.shape[1]
    batches = slots // BATCH
    return pl.pallas_call(
        gather_body,
        grid_spec=pltpu.PrefetchScalarGridSpec(
            num_scalar_prefetch=1,
            grid=(1,),
            in_specs=[pl.BlockSpec(memory_space=pl.ANY)],
            out_specs=pl.BlockSpec((slots, width), lambda i, _: (0, 0)),
            scratch_shapes=[
                pltpu.VMEM((batches, BATCH * 16, width), embed.dtype),
                pltpu.VMEM((8, 16, width), jnp.float32),
                pltpu.VMEM((slots, width), jnp.float32),
                pltpu.SemaphoreType.DMA((batches,)),
            ],
        ),
        out_shape=jax.ShapeDtypeStruct((slots, width), embed.dtype),
        compiler_params=pltpu.CompilerParams(vmem_limit_bytes=56 * 2**20),
        cost_estimate=pl.CostEstimate(
            flops=0, bytes_accessed=40 * slots * width, transcendentals=0
        ),
    )(ids, embed)


def attend_body(lengths, fresh, keys, values, heads):
    rows, groups, _, width = fresh.shape
    lines, places = QG * STEPS, keys.shape[1]
    scale = width ** (-0.5)
    start = pl.program_id(0) * rows
    column = lax.broadcasted_iota(jnp.int32, (lines, places), 1)
    step_of = lax.broadcasted_iota(jnp.int32, (lines, 2 * STEPS), 0) % STEPS
    turn = lax.broadcasted_iota(jnp.int32, (lines, 2 * STEPS), 1) - STEPS
    causal = (turn >= 0) & (turn <= step_of)
    across = (((1,), (1,)), ((), ()))
    scores = []
    for row in range(rows):
        live = column < lengths[start + row]
        for group in range(groups):
            at = slice(group * width, (group + 1) * width)
            query = fresh[row, group, :lines]
            both = fresh[row, group, lines:]
            turned = pltpu.roll(both.astype(jnp.float32), STEPS, axis=0).astype(jnp.bfloat16)
            cached = lax.dot_general(
                query, keys[row, :, at], across, preferred_element_type=jnp.float32
            )
            new = lax.dot_general(query, turned, across, preferred_element_type=jnp.float32)
            cached = jnp.where(live, cached * scale, masked_score)
            new = jnp.where(causal, new * scale, masked_score)
            scores.append((cached, new, both))
    probs = []
    for cached, new, both in scores:
        top = jnp.maximum(
            jnp.max(cached, axis=-1, keepdims=True), jnp.max(new, axis=-1, keepdims=True)
        )
        cached = jnp.exp(cached - top)
        new = jnp.exp(new - top)
        total = jnp.sum(cached, axis=-1, keepdims=True) + jnp.sum(new, axis=-1, keepdims=True)
        share = 1.0 / total
        probs.append(
            ((cached * share).astype(jnp.bfloat16), (new * share).astype(jnp.bfloat16), both)
        )
    for row in range(rows):
        for group in range(groups):
            at = slice(group * width, (group + 1) * width)
            cached, new, both = probs[row * groups + group]
            out = jnp.dot(cached, values[row, :, at], preferred_element_type=jnp.float32)
            out = out + jnp.dot(new, both, preferred_element_type=jnp.float32)
            heads[row, group] = out.astype(jnp.bfloat16)


def attend(projected, keys, values, lengths):
    count, columns = projected.shape
    groups = columns // INNER
    here = count // STEPS
    rows = min(ATTEND_ROWS, here)
    lines = STEPS * QG
    fresh = projected.reshape(here, STEPS, groups, QG + 2, HEAD_SIZE).transpose(0, 2, 3, 1, 4)
    fresh = fresh.reshape(here, groups, lines + 2 * STEPS, HEAD_SIZE)
    places, width = keys.shape[1:]
    cache = pl.BlockSpec((rows, places, width), lambda i, _: (i, 0, 0))
    heads = pl.pallas_call(
        attend_body,
        grid_spec=pltpu.PrefetchScalarGridSpec(
            num_scalar_prefetch=1,
            grid=(here // rows,),
            in_specs=[
                pl.BlockSpec((rows,) + fresh.shape[1:], lambda i, _: (i, 0, 0, 0)),
                cache,
                cache,
            ],
            out_specs=pl.BlockSpec((rows, groups, lines, HEAD_SIZE), lambda i, _: (i, 0, 0, 0)),
        ),
        out_shape=jax.ShapeDtypeStruct((here, groups, lines, HEAD_SIZE), jnp.bfloat16),
        compiler_params=pltpu.CompilerParams(vmem_limit_bytes=56 * 2**20),
        cost_estimate=pl.CostEstimate(
            flops=4 * here * groups * lines * places * HEAD_SIZE,
            bytes_accessed=4 * here * places * width,
            transcendentals=here * groups * lines * places,
        ),
    )(lengths, fresh, keys, values)
    heads = heads.reshape(here, groups, QG, STEPS, HEAD_SIZE).transpose(1, 2, 4, 0, 3)
    return heads.reshape(groups * OUTER, count)


def flip(values, axis, bit):
    n = lax.axis_size(axis)
    return lax.ppermute(values, axis, [(i, i ^ bit) for i in range(n)])


def hop(values, first, last, step):
    pairs = [(2 * p + core, 2 * (p + step) + core) for p in range(first, last) for core in (0, 1)]
    return lax.ppermute(values, "rep", pairs)


def block_of(values, index):
    return lax.dynamic_index_in_dim(values, index, 0, keepdims=False)


def outward_body(weights, heads, out):
    found = jnp.dot(weights[...], heads[...], preferred_element_type=jnp.float32)
    out[0] = found.astype(out.dtype)


def outward(weights, heads, blocks):
    depth, count = heads.shape
    width = weights.shape[0] // blocks
    return pl.pallas_call(
        outward_body,
        grid=(blocks,),
        in_specs=[
            pl.BlockSpec((width, depth), lambda i: (i, 0)),
            pl.BlockSpec((depth, count), lambda i: (0, 0)),
        ],
        out_specs=pl.BlockSpec((1, width, count), lambda i: (i, 0, 0)),
        out_shape=jax.ShapeDtypeStruct((blocks, width, count), jnp.bfloat16),
        compiler_params=pltpu.CompilerParams(vmem_limit_bytes=56 * 2**20),
        cost_estimate=pl.CostEstimate(
            flops=2 * count * depth * width * blocks,
            bytes_accessed=2 * depth * width * blocks,
            transcendentals=0,
        ),
    )(weights, heads)


def project_body(slots, here, there, inner_here, inner_there, out):
    rows = here.shape[0]
    column = lax.broadcasted_iota(jnp.int32, (slots.shape[0], rows), 1)
    pick = (column == slots[...]).astype(jnp.bfloat16)
    dot = functools.partial(jnp.dot, preferred_element_type=jnp.float32)
    first = dot(pick, here[...]).astype(jnp.bfloat16)
    second = dot(pick, there[...]).astype(jnp.bfloat16)
    out[...] = dot(first, inner_here[...]) + dot(second, inner_there[...])


def project(slots, here, there, inner_here, inner_there, planes):
    total = slots.shape[0]
    count = total // PROJECT_STEPS
    rows, depth = here.shape
    columns = inner_here.shape[1]
    all_of = lambda shape: pl.BlockSpec(shape, lambda i: (0, 0))
    return pl.pallas_call(
        project_body,
        grid=(PROJECT_STEPS,),
        in_specs=[pl.BlockSpec((count, 1), lambda i: (i, 0))]
        + [all_of((rows, depth))] * 2
        + [all_of((depth, columns))] * 2,
        out_specs=pl.BlockSpec((count, columns), lambda i: (i, 0)),
        out_shape=jax.ShapeDtypeStruct((total, columns), jnp.float32),
        compiler_params=pltpu.CompilerParams(vmem_limit_bytes=56 * 2**20),
        cost_estimate=pl.CostEstimate(
            flops=4 * total * depth * (rows + columns),
            bytes_accessed=4 * (rows + columns) * depth + 4 * total * columns,
            transcendentals=0,
        ),
    )(slots, here, there, inner_here, inner_there).reshape(planes, -1, columns)


def tie(values, *others):
    return lax.optimization_barrier((values, others))


def line_sum(terms, plane, planes, late):
    width = terms.shape[2] // SUM_PARTS
    block = lambda d, part: lax.dynamic_slice(
        terms, (d, 0, part * width), (1, terms.shape[1], width)
    )[0]
    right, left = [None] * SUM_PARTS, [None] * SUM_PARTS
    for step in range(1, planes):
        for part in range(SUM_PARTS):
            forth = block(jnp.minimum(plane + planes - step, planes - 1), part)
            back = block(jnp.maximum(plane - planes + step, 0), part)
            if step > 1:
                forth, back = forth + right[part], back + left[part]
            right[part] = hop(forth.astype(jnp.bfloat16), 0, step, 1)
            left[part] = hop(back.astype(jnp.bfloat16), planes - step, planes, -1)
        if step == max(planes - 2, 1):
            (right, left), (late,) = tie((right, left), late)
    sums = [
        block(plane, part) + right[part].astype(jnp.float32) + left[part].astype(jnp.float32)
        for part in range(SUM_PARTS)
    ]
    return jnp.concatenate(sums, axis=1), late


def leaders(ids):
    count = ids.shape[-1]
    index = jnp.arange(count, dtype=jnp.int32)
    same = ids[..., :, None] == ids[..., None, :]
    leader = jnp.min(jnp.where(same, index[:, None], count), axis=-2)
    return leader, leader == index


def numbers(block, leader, first):
    index = jnp.arange(block.shape[-1], dtype=jnp.int32)
    ahead = (block[..., :, None] == block[..., None, :]) & first[..., :, None]
    ahead = ahead & (index[:, None] < leader[..., None, :])
    return jnp.sum(ahead.astype(jnp.int32), axis=-2)


def listed(values, chosen, number, low, slots):
    at = jnp.where(chosen, number - low, -1)
    hit = at[..., :, None] == jnp.arange(slots, dtype=jnp.int32)
    return jnp.sum(jnp.where(hit, values[..., :, None], 0), axis=-2)


def slot_of(block, number, low, slots):
    slot = number - low
    return jnp.where((slot >= 0) & (slot < slots), block * slots + slot, -1)


def picked(slot, rows):
    pick = slot[:, None] == jnp.arange(rows.shape[0], dtype=jnp.int32)[None, :]
    return jnp.dot(pick.astype(jnp.bfloat16), rows, preferred_element_type=jnp.float32).astype(
        jnp.bfloat16
    )


def exchange(blocks, axis, place):
    n = blocks.shape[0]
    out = lax.dynamic_update_index_in_dim(blocks, block_of(blocks, place), place, 0)
    for mask in range(1, n):
        got = flip(block_of(blocks, place ^ mask), axis, mask)
        early = got if mask == 1 else early
        out = lax.dynamic_update_index_in_dim(out, got, place ^ mask, 0)
    return out, early


def shards(
    master,
    first_moment,
    second_moment,
    grads,
    embed,
    ln_gain,
    post_gain,
    cache_keys,
    stored_values,
    lengths,
    token_ids,
):
    n_rep = lax.axis_size("rep")
    n_tp = lax.axis_size("tp")
    rep, tp = lax.axis_index("rep"), lax.axis_index("tp")
    planes = n_rep // 2
    plane, core = rep // 2, rep % 2
    vocab_local, width_local = embed.shape
    rows_here = lengths.shape[0]
    count = rows_here * STEPS
    depth = MODEL_WIDTH // n_rep
    swap = lambda values, axis="tp": lax.all_to_all(
        values, axis, split_axis=0, concat_axis=0, tiled=True
    )

    ids = token_ids.reshape(n_rep, count)
    block = ids // vocab_local
    flat_ids, flat_block = ids.reshape(-1), block.reshape(-1)
    leader, first = leaders(flat_ids)
    mine = first & (flat_block == rep)
    index = jnp.arange(flat_ids.shape[0], dtype=jnp.int32)
    place = jnp.sum((mine[:, None] & (index[:, None] < index[None, :])).astype(jnp.int32), axis=0)
    local_ids = flat_ids - rep * vocab_local
    fetch = lambda turn: gather_rows(embed, listed(local_ids, mine, place, turn * SLOTS, SLOTS))
    rows = fetch(0)
    swapped = swap(rows.reshape(n_tp, -1, width_local))

    weights_in = (master, first_moment, second_moment, grads)
    weights_in, _ = tie(weights_in, rows)
    *partial, outer = adam(weights_in, (), n_tp, INNER, OUTER)
    swapped, (outer,) = tie(swapped, outer)
    outer = exchange(outer, "tp", tp)[0].reshape(depth, -1)
    out_weights = lax.all_gather(outer, "rep", axis=0, tiled=True)

    def normed_rows(found):
        tokens = found.astype(jnp.float32)
        mean_sq = jnp.sum(tokens * tokens, axis=(0, 2), keepdims=True) / MODEL_WIDTH
        normed_in = tokens * lax.rsqrt(mean_sq + norm_eps) * ln_gain.reshape(n_tp, 1, width_local)
        normed_in = normed_in.astype(jnp.bfloat16)
        share = normed_in.shape[1]
        normed_in = normed_in.reshape(n_tp, share, n_rep // n_tp, depth).transpose(0, 2, 1, 3)
        return normed_in.reshape(n_rep, share, depth)

    def all_slots(got):
        got = got.reshape(-1, depth)
        return jnp.concatenate([got] + [flip(got, "tp", mask) for mask in range(1, n_tp)])

    def slot_from(block, number, low):
        slot = number - low
        share = SLOTS // n_tp
        at = ((slot // share) ^ tp) * n_rep * share + block * share + slot % share
        return jnp.where((slot >= 0) & (slot < SLOTS), at, -1)

    normed_in = normed_rows(swapped)
    got = swap(normed_in, "rep")
    (weights_in, partial), _ = tie((weights_in, partial), normed_in)
    updated, new_first, second, inner = adam(weights_in, partial, n_tp, 0, INNER)
    got, (inner,) = tie(got, inner)
    inner, first_flip = exchange(inner, "tp", tp)
    got, _ = tie(got, first_flip)
    inner = inner.reshape(depth, -1)
    inner_other = flip(inner, "rep", 1)

    here = all_slots(got)
    flat_block, _ = tie(flat_block, got)
    number = numbers(flat_block, leader, first)
    core_tokens = lambda values: lax.dynamic_index_in_dim(
        values.reshape(planes, 2, count), core, 1, keepdims=False
    ).reshape(-1)
    core_block, core_number = core_tokens(flat_block), core_tokens(number)
    rounds = jnp.max(number) // SLOTS + 1
    slot_at = lambda turn: slot_from(core_block, core_number, turn * SLOTS)[:, None]
    here, (first_slots, rounds) = tie(here, slot_at(0), rounds)

    def terms_of(here, slots):
        return project(slots, here, flip(here, "rep", 1), inner, inner_other, planes)

    def terms_again(turn):
        found = swap(fetch(turn).reshape(n_tp, -1, width_local))
        return terms_of(all_slots(swap(normed_rows(found), "rep")), slot_at(turn))

    terms = terms_of(here, first_slots)
    terms = lax.fori_loop(1, rounds, lambda turn, kept: kept + terms_again(turn), terms)

    ids, _ = tie(ids, terms)
    row_leader, row_first = leaders(ids)
    row_number = numbers(block, row_leader, row_first)
    my_block, my_number = block_of(block, rep), block_of(row_number, rep)

    def to_send(far, near, found):
        low = far * ROW_SLOTS
        chosen = row_first & (block == rep)
        of = listed(number.reshape(n_rep, -1) + 1, chosen, row_number, low, ROW_SLOTS)
        slot = slot_of(0, of.reshape(-1) - 1, near * SLOTS, SLOTS)
        return picked(slot, found).reshape(n_rep, ROW_SLOTS, width_local)

    def own_rows(far, sent):
        found = exchange(sent, "rep", rep)[0].reshape(-1, width_local)
        return picked(slot_of(my_block, my_number, far * ROW_SLOTS, ROW_SLOTS), found)

    sent = to_send(0, 0, rows)
    projected, (out_weights, sent) = line_sum(terms, plane, planes, (out_weights, sent))
    projected = projected.astype(jnp.bfloat16)
    heads = attend(projected, cache_keys, stored_values, lengths)
    partial_out = outward(out_weights, heads, 2).reshape(n_tp, width_local, count)
    attended = swap(partial_out)
    sent, _ = tie(sent, partial_out)
    own_cols = own_rows(0, sent)
    attended, (own_cols,) = tie(attended, own_cols)
    own_cols = lax.fori_loop(
        1,
        (jnp.max(row_number) // ROW_SLOTS + 1) * rounds,
        lambda turn, kept: kept
        + own_rows(
            turn // rounds, to_send(turn // rounds, turn % rounds, fetch(turn % rounds))
        ),
        own_cols,
    )
    attended = jnp.sum(attended.astype(jnp.float32), axis=0).T
    resid = own_cols.astype(jnp.float32) + attended
    square = jnp.sum(resid * resid, axis=-1)
    total = functools.reduce(
        jnp.add, [square] + [flip(square, "tp", other) for other in range(1, n_tp)]
    )
    gain = lax.dynamic_slice_in_dim(post_gain, tp * width_local, width_local, 0)
    normed = resid * lax.rsqrt(total / MODEL_WIDTH + norm_eps)[:, None] * gain
    normed = normed.astype(jnp.bfloat16).reshape(rows_here, STEPS, width_local)
    return (updated, new_first, second, normed)


def solution(mesh):
    return jax.shard_map(
        shards,
        mesh=mesh,
        in_specs=(
            P(("rep", "tp"), None),
            P(("rep", "tp"), None),
            P(("rep", "tp"), None),
            P(("rep", "tp"), None),
            P("rep", "tp"),
            P(),
            P(),
            P("rep", None, "tp"),
            P("rep", None, "tp"),
            P("rep"),
            P(),
        ),
        out_specs=(
            P(("rep", "tp"), None),
            P(("rep", "tp"), None),
            P(("rep", "tp"), None),
            P("rep", None, "tp"),
        ),
        check_vma=False,
    )
```
